512 devices in a mesh: row: 16 (over y, x), col: 16 (over z), depth: 2 (over core).
Axes of the slice: x: 4, y: 4, z: 16, core: 2. Of those that a mesh axis runs over, the one named last changes fastest.
Arguments:
- a_matrix: bfloat16 [8192, 8192], P('row', 'col'), may hold values from -6 to 6
- b_matrix: bfloat16 [8192, 8192], P('row', 'col'), may hold values from -0.0625 to 0.0625
- mask_a: int32 [64, 64], P('row', 'col'), may hold values from 0 to 1, as said below
- mask_b: int32 [64, 64], P('row', 'col'), may hold values from 0 to 1, as said below
Outputs:
- product: bfloat16 [8192, 8192], P('row', ('col', 'depth'))
- rms_norm: float32 [], replicated
The draws below stay inside these ranges and needn't reach their ends.
Inputs may be any that keep to these rules, and one draw needn't show every extreme that they name: `mask_a`: 1 marks an occupied block; occupancy thins out with distance from the diagonal, and every diagonal block is occupied. `mask_b`: 1 marks an occupied block; occupancy thins out with distance from the diagonal, and every diagonal block is occupied.
All inputs are finite; a program needn't handle non-finite values.
Results may differ from the reference program's by a relative error of at most 0.001.
Values may be sent and summed in bfloat16 or wider, within the bound.
No kernel may reach another device: no remote copies, remote signals or barrier semaphores. Data moves between devices by JAX's collectives and lax.ppermute only.
A program may use at most 64 MiB of HBM per device.

```python
import jax
import jax.numpy as jnp

BLK = 128
NB = 64
N = 8192


def band_mask(key):
    rows = jnp.arange(NB, dtype=jnp.int32)[:, None]
    cols = jnp.arange(NB, dtype=jnp.int32)[None, :]
    distance = jnp.abs(rows - cols)
    limit = 8 - 7 * distance // NB
    rolled = jax.random.randint(key, (NB, NB), 0, 8, dtype=jnp.int32)
    return (rolled < limit).astype(jnp.int32)


def draw_mask_a(key, part):
    key = jax.random.fold_in(key, 11)
    return band_mask(key)


def draw_mask_b(key, part):
    key = jax.random.fold_in(key, 23)
    return band_mask(key)


def block_scale(own_key, shape, split, smallest, high):
    gain, own = 1.0, jax.random.fold_in(own_key, 6)
    for dim, parts in split:
        steps = jnp.exp(jax.random.uniform(jax.random.fold_in(own, dim), (parts,), jnp.float32, smallest / len(split), high / len(split)))
        gain = gain * jnp.repeat(steps, shape[dim] // parts).reshape([-1 if axis == dim else 1 for axis in range(len(shape))])
    return gain


def gaussian(own_key, shape, deviation, most, cuts=(), held_as=jnp.bfloat16):
    entries = jax.random.normal(own_key, shape, jnp.float32) * deviation
    if len(cuts) > 0:
        entries = block_scale(own_key, shape, cuts, -0.22, 0.18) * entries
    return jnp.clip(entries, min=-most, max=most).astype(held_as)


def setup_inputs(seed: int = 0) -> dict:
    splits = jax.random.split(jax.random.key(seed), 5)
    a_matrix = gaussian(splits[0], (N, N), 1.0, 6.0, ((0, 16), (1, 16)))
    b_matrix = gaussian(splits[1], (N, N), N ** -0.5, 0.0625, ((0, 16), (1, 16)))
    mask_a = draw_mask_a(jax.random.fold_in(splits[4], 71), 0)
    mask_b = draw_mask_b(jax.random.fold_in(splits[4], 71), 0)
    return {"a_matrix": a_matrix, "b_matrix": b_matrix, "mask_a": mask_a, "mask_b": mask_b}


def apply_mask(matrix, mask):
    blocks = mask.shape[0]
    shaped = matrix.reshape(blocks, BLK, blocks, BLK) * mask.astype(matrix.dtype)[:, None, :, None]
    return shaped.reshape(matrix.shape)

def reference(a_matrix, b_matrix, mask_a, mask_b):
    left = apply_mask(a_matrix, mask_a)
    right = apply_mask(b_matrix, mask_b)
    full = jnp.dot(left, right, preferred_element_type=jnp.float32)
    rms_norm = jnp.sqrt(jnp.mean(full * full) + 1e-06)
    return (full.astype(jnp.bfloat16), rms_norm)
```

```python
import functools

import jax
import jax.numpy as jnp
from jax import lax
from jax.experimental import pallas as pl
from jax.experimental.pallas import tpu as pltpu
from jax.sharding import PartitionSpec as P


def apply_mask(panel, mask):
    blocks_r, blocks_c = mask.shape
    size_r = panel.shape[0] // blocks_r
    size_c = panel.shape[1] // blocks_c
    spread = jnp.repeat(jnp.repeat(mask, size_r, 0), size_c, 1)
    return jnp.where(spread != 0, panel, jnp.zeros_like(panel))


def product_kernel(a_ref, b_ref, mine_ref, theirs_ref):
    step = pl.program_id(0)
    half = mine_ref.shape[1]
    part = jnp.dot(a_ref[0], b_ref[0], preferred_element_type=jnp.float32)

    @pl.when(step == 0)
    def _():
        mine_ref[...] = part[:, :half]
        theirs_ref[...] = part[:, half:]

    @pl.when(step > 0)
    def _():
        mine_ref[...] += part[:, :half]
        theirs_ref[...] += part[:, half:]


def multiply(a_all, b_all):
    count, rows, depth = a_all.shape
    cols = b_all.shape[2]
    half = jax.ShapeDtypeStruct((rows, cols // 2), jnp.float32)
    spec = pl.BlockSpec((rows, cols // 2), lambda s: (0, 0))
    return pl.pallas_call(
        product_kernel,
        grid=(count,),
        in_specs=[
            pl.BlockSpec((1, rows, depth), lambda s: (s, 0, 0)),
            pl.BlockSpec((1, depth, cols), lambda s: (s, 0, 0)),
        ],
        out_specs=[spec, spec],
        out_shape=[half, half],
        compiler_params=pltpu.CompilerParams(vmem_limit_bytes=24 << 20),
        cost_estimate=pl.CostEstimate(
            flops=2 * count * rows * depth * cols,
            bytes_accessed=a_all.size * 2 + b_all.size * 2 + rows * cols * 4,
            transcendentals=0,
        ),
    )(a_all, b_all)


def per_device(a_matrix, b_matrix, mask_a, mask_b):
    layer = lax.axis_index("depth")
    layers = lax.axis_size("depth")
    count = lax.axis_size("row")
    width = a_matrix.shape[0]
    share = width // layers
    masked_a = apply_mask(a_matrix, mask_a)
    masked_b = apply_mask(b_matrix, mask_b)
    a_part = lax.dynamic_slice_in_dim(masked_a, layer * share, share, 1)
    b_part = lax.dynamic_slice_in_dim(masked_b, layer * share, share, 0)
    b_part = jnp.where(
        layer == 0, b_part, jnp.concatenate([b_part[:, share:], b_part[:, :share]], 1)
    )
    a_all = lax.all_gather(a_part, "col", axis=0)
    b_all = lax.all_gather(b_part, "row", axis=0)
    mine, theirs = multiply(a_all, b_all)
    other = lax.ppermute(theirs, "depth", [(0, 1), (1, 0)])
    full = mine + other
    squares = lax.psum(jnp.sum(full * full), ("row", "col", "depth"))
    entries = float(width * count * (width * count))
    rms_norm = jnp.sqrt(squares / entries + 1e-06)
    return (full.astype(jnp.bfloat16), rms_norm)


def solution(mesh):
    placed = (P("row", "col"), P("row", "col"), P("row", "col"), P("row", "col"))
    return jax.shard_map(
        per_device,
        mesh=mesh,
        in_specs=placed,
        out_specs=(P("row", ("col", "depth")), P()),
        check_vma=False,
    )
```

```python
import jax
import jax.numpy as jnp
from jax import lax
from jax.experimental import pallas as pl
from jax.experimental.pallas import tpu as pltpu
from jax.sharding import PartitionSpec as P


def mask_kernel(layer_ref, mask_a_ref, mask_b_ref, a_ref, b_ref, a_out, b_out):
    layer = layer_ref[0]
    blocks = mask_a_ref.shape[0]
    size = a_ref.shape[0] // blocks
    half = blocks // 2
    share = half * size
    for d in range(2):
        @pl.when(layer == d)
        def _(d=d):
            for i in range(blocks):
                for j in range(half):
                    k = d * half + j
                    tile = a_ref[i * size:(i + 1) * size, k * size:(k + 1) * size]
                    keep = mask_a_ref[i, k] != 0
                    a_out[i * size:(i + 1) * size, j * size:(j + 1) * size] = jnp.where(
                        keep, tile, jnp.zeros_like(tile)
                    )
                    c = (i * size + d * share) % (2 * share)
                    tile = b_ref[k * size:(k + 1) * size, i * size:(i + 1) * size]
                    keep = mask_b_ref[k, i] != 0
                    b_out[j * size:(j + 1) * size, c:c + size] = jnp.where(
                        keep, tile, jnp.zeros_like(tile)
                    )


def mask_parts(layer, mask_a, mask_b, a_matrix, b_matrix):
    width = a_matrix.shape[0]
    smem = pl.BlockSpec(memory_space=pltpu.SMEM)
    vmem = pl.BlockSpec(memory_space=pltpu.VMEM)
    return pl.pallas_call(
        mask_kernel,
        in_specs=[smem, smem, smem, vmem, vmem],
        out_specs=[vmem, vmem],
        out_shape=[
            jax.ShapeDtypeStruct((width, width // 2), a_matrix.dtype),
            jax.ShapeDtypeStruct((width // 2, width), b_matrix.dtype),
        ],
        compiler_params=pltpu.CompilerParams(vmem_limit_bytes=16 << 20),
    )(layer[None], mask_a, mask_b, a_matrix, b_matrix)


def product_kernel(a_ref, b_ref, mine_ref, theirs_ref):
    step = pl.program_id(0)
    half = mine_ref.shape[1]
    part = jnp.dot(a_ref[0], b_ref[0], preferred_element_type=jnp.float32)
    for s in range(1, a_ref.shape[0]):
        part += jnp.dot(a_ref[s], b_ref[s], preferred_element_type=jnp.float32)

    @pl.when(step == 0)
    def _():
        mine_ref[...] = part[:, :half]
        theirs_ref[...] = part[:, half:]

    @pl.when(step > 0)
    def _():
        mine_ref[...] += part[:, :half]
        theirs_ref[...] += part[:, half:]


def multiply(a_all, b_all, group=4):
    count, rows, depth = a_all.shape
    cols = b_all.shape[2]
    half = jax.ShapeDtypeStruct((rows, cols // 2), jnp.float32)
    spec = pl.BlockSpec((rows, cols // 2), lambda s: (0, 0))
    return pl.pallas_call(
        product_kernel,
        grid=(count // group,),
        in_specs=[
            pl.BlockSpec((group, rows, depth), lambda s: (s, 0, 0)),
            pl.BlockSpec((group, depth, cols), lambda s: (s, 0, 0)),
        ],
        out_specs=[spec, spec],
        out_shape=[half, half],
        compiler_params=pltpu.CompilerParams(vmem_limit_bytes=56 << 20),
        cost_estimate=pl.CostEstimate(
            flops=2 * count * rows * depth * cols,
            bytes_accessed=a_all.size * 2 + b_all.size * 2 + rows * cols * 4,
            transcendentals=0,
        ),
    )(a_all, b_all)


def total_over(value, axis, size):
    copies = jnp.broadcast_to(value, (size,) + value.shape)
    return jnp.sum(lax.all_to_all(copies, axis, 0, 0, tiled=True), 0)


def per_device(a_matrix, b_matrix, mask_a, mask_b):
    layer = lax.axis_index("depth")
    layers = lax.axis_size("depth")
    count = lax.axis_size("row")
    width = a_matrix.shape[0]
    a_part, b_part = mask_parts(layer, mask_a, mask_b, a_matrix, b_matrix)
    a_all = lax.all_gather(a_part, "col", axis=0)
    copies = jnp.broadcast_to(b_part, (count,) + b_part.shape)
    b_all = lax.all_to_all(copies, "row", 0, 0, tiled=True)
    mine, theirs = multiply(a_all, b_all)
    other = lax.ppermute(theirs, "depth", [(0, 1), (1, 0)])
    full = mine + other
    squares = jnp.sum(jnp.square(full).reshape(-1, 1, 128), 0)
    squares = total_over(squares, ("row", "depth"), count * layers)
    near = [[4 * g + i for i in range(4)] for g in range(count // 4)]
    far = [[4 * g + i for g in range(count // 4)] for i in range(4)]
    for groups in (near, far):
        squares = jnp.sum(lax.all_gather(squares, "col", axis_index_groups=groups), 0)
    entries = float(width * count * (width * count))
    rms_norm = jnp.sqrt(jnp.sum(squares) / entries + 1e-06)
    return (full.astype(jnp.bfloat16), rms_norm)


def solution(mesh):
    placed = (P("row", "col"), P("row", "col"), P("row", "col"), P("row", "col"))
    return jax.shard_map(
        per_device,
        mesh=mesh,
        in_specs=placed,
        out_specs=(P("row", ("col", "depth")), P()),
        check_vma=False,
    )
```

```python
import jax
import jax.numpy as jnp
from jax import lax
from jax.experimental import pallas as pl
from jax.experimental.pallas import tpu as pltpu
from jax.sharding import PartitionSpec as P


def mask_kernel(layer_ref, mask_ref, matrix_ref, out_ref):
    blocks = mask_ref.shape[0]
    size = matrix_ref.shape[0] // blocks
    half = blocks // 2
    layer = layer_ref[0]
    for d in range(2):
        @pl.when(layer == d)
        def _(d=d):
            for i in range(blocks):
                for j in range(half):
                    k = d * half + j
                    tile = matrix_ref[i * size:(i + 1) * size, k * size:(k + 1) * size]
                    out_ref[i * size:(i + 1) * size, j * size:(j + 1) * size] = jnp.where(
                        mask_ref[i, k] != 0, tile, jnp.zeros_like(tile)
                    )


def masked_half(layer, mask, matrix):
    width = matrix.shape[0]
    smem = pl.BlockSpec(memory_space=pltpu.SMEM)
    vmem = pl.BlockSpec(memory_space=pltpu.VMEM)
    return pl.pallas_call(
        mask_kernel,
        in_specs=[smem, smem, vmem],
        out_specs=vmem,
        out_shape=jax.ShapeDtypeStruct((width, width // 2), matrix.dtype),
        compiler_params=pltpu.CompilerParams(vmem_limit_bytes=58 << 20),
        cost_estimate=pl.CostEstimate(
            flops=0, bytes_accessed=matrix.size * 3, transcendentals=0
        ),
    )(layer[None], mask, matrix)


def total_over(value, axis, size):
    copies = jnp.broadcast_to(value, (size,) + value.shape)
    return jnp.sum(lax.all_to_all(copies, axis, 0, 0, tiled=True), 0)


def per_device(a_matrix, b_matrix, mask_a, mask_b):
    layer = lax.axis_index("depth")
    layers = lax.axis_size("depth")
    count = lax.axis_size("row")
    width = a_matrix.shape[0]
    share = width // layers
    a_part = masked_half(layer, mask_a, a_matrix)
    a_all = lax.all_gather(a_part, ("col", "depth"), axis=0)
    b_part = masked_half(layer, mask_b, b_matrix)
    copies = jnp.broadcast_to(b_part, (count,) + b_part.shape)
    b_all = lax.all_to_all(copies, "row", 0, 0, tiled=True)
    b_all = b_all.reshape(count * layers, share, share)
    full = jnp.einsum("smk,skn->mn", a_all, b_all, preferred_element_type=jnp.float32)
    squares = jnp.sum(jnp.square(full).reshape(-1, 1, 128), 0)
    squares = total_over(squares, ("row", "depth"), count * layers)
    near = [[4 * g + i for i in range(4)] for g in range(count // 4)]
    far = [[4 * g + i for g in range(count // 4)] for i in range(4)]
    for groups in (near, far):
        squares = jnp.sum(lax.all_gather(squares, "col", axis_index_groups=groups), 0)
    entries = float(width * count * (width * count))
    rms_norm = jnp.sqrt(jnp.sum(squares) / entries + 1e-06)
    return (full.astype(jnp.bfloat16), rms_norm)


def solution(mesh):
    placed = (P("row", "col"), P("row", "col"), P("row", "col"), P("row", "col"))
    return jax.shard_map(
        per_device,
        mesh=mesh,
        in_specs=placed,
        out_specs=(P("row", ("col", "depth")), P()),
        check_vma=False,
    )
```

```python
import functools

import jax
import jax.numpy as jnp
from jax import lax
from jax.experimental import pallas as pl
from jax.experimental.pallas import tpu as pltpu
from jax.sharding import PartitionSpec as P


def mask_kernel(layer_ref, mask_ref, matrix_ref, out_ref):
    blocks = mask_ref.shape[0]
    size = matrix_ref.shape[0] // blocks
    half = blocks // 2
    layer = layer_ref[0]
    for d in range(2):
        @pl.when(layer == d)
        def _(d=d):
            for i in range(blocks):
                for j in range(half):
                    k = d * half + j
                    tile = matrix_ref[i * size:(i + 1) * size, k * size:(k + 1) * size]
                    out_ref[i * size:(i + 1) * size, j * size:(j + 1) * size] = jnp.where(
                        mask_ref[i, k] != 0, tile, jnp.zeros_like(tile)
                    )


def masked_half(layer, mask, matrix):
    width = matrix.shape[0]
    smem = pl.BlockSpec(memory_space=pltpu.SMEM)
    vmem = pl.BlockSpec(memory_space=pltpu.VMEM)
    return pl.pallas_call(
        mask_kernel,
        in_specs=[smem, smem, vmem],
        out_specs=vmem,
        out_shape=jax.ShapeDtypeStruct((width, width // 2), matrix.dtype),
        compiler_params=pltpu.CompilerParams(vmem_limit_bytes=58 << 20),
        cost_estimate=pl.CostEstimate(
            flops=0, bytes_accessed=matrix.size * 3, transcendentals=0
        ),
    )(layer[None], mask, matrix)


def product_kernel(ahead, a_ref, b_ref, out_ref, squares_ref, a_held, b_held, a_came, b_came):
    count = a_ref.shape[0]

    def copies(n):
        return (
            pltpu.make_async_copy(b_ref.at[n], b_held.at[n], b_came.at[n]),
            pltpu.make_async_copy(a_ref.at[n], a_held.at[n], a_came.at[n]),
        )

    for n in range(min(ahead, count)):
        for copy in copies(n):
            copy.start()
    total = None
    for n in range(count):
        for copy in copies(n):
            copy.wait()
        if n + ahead < count:
            for copy in copies(n + ahead):
                copy.start()
        part = jnp.dot(a_held[n], b_held[n], preferred_element_type=jnp.float32)
        total = part if total is None else total + part
    out_ref[...] = total.astype(out_ref.dtype)
    squares = jnp.sum(jnp.square(total).reshape(-1, 8, total.shape[1]), 0)
    squares_ref[...] = jnp.sum(squares[:, :128] + squares[:, 128:], 0, keepdims=True)


def multiply(a_all, b_all):
    count, rows, depth = a_all.shape
    cols = b_all.shape[2]
    vmem = pl.BlockSpec(memory_space=pltpu.VMEM)
    hbm = pl.BlockSpec(memory_space=pl.ANY)
    return pl.pallas_call(
        functools.partial(product_kernel, 8),
        in_specs=[hbm, hbm],
        out_specs=[vmem, vmem],
        out_shape=[
            jax.ShapeDtypeStruct((rows, cols), a_all.dtype),
            jax.ShapeDtypeStruct((1, 128), jnp.float32),
        ],
        scratch_shapes=[
            pltpu.VMEM(a_all.shape, a_all.dtype),
            pltpu.VMEM(b_all.shape, b_all.dtype),
            pltpu.SemaphoreType.DMA((count,)),
            pltpu.SemaphoreType.DMA((count,)),
        ],
        compiler_params=pltpu.CompilerParams(vmem_limit_bytes=57 << 20),
        cost_estimate=pl.CostEstimate(
            flops=2 * count * rows * depth * cols,
            bytes_accessed=2 * (a_all.size + b_all.size),
            transcendentals=0,
        ),
    )(a_all, b_all)


def total_over_all(value, count, layers, near=4):
    far = count // near
    runs = [
        [(r * count + run * near + c) * layers + d
         for r in range(count) for c in range(near) for d in range(layers)]
        for run in range(far)
    ]
    copies = jnp.broadcast_to(value, (len(runs[0]),) + value.shape)
    value = jnp.sum(
        lax.all_to_all(
            copies, ("row", "col", "depth"), 0, 0, tiled=True, axis_index_groups=runs
        ), 0
    )
    apart = [[run * near + c for run in range(far)] for c in range(near)]
    return jnp.sum(lax.all_gather(value, "col", axis_index_groups=apart), (0, 1, 2))


def per_device(a_matrix, b_matrix, mask_a, mask_b):
    layer = lax.axis_index("depth")
    layers = lax.axis_size("depth")
    count = lax.axis_size("row")
    width = a_matrix.shape[0]
    a_part = masked_half(layer, mask_a, a_matrix)
    a_all = lax.all_gather(a_part, ("col", "depth"), axis=0)
    b_part = masked_half(layer, mask_b, b_matrix)
    copies = jnp.broadcast_to(b_part, (count,) + b_part.shape)
    b_all = lax.all_to_all(copies, "row", 0, 0, tiled=True)
    product, squares = multiply(a_all, b_all.reshape(a_all.shape[0], -1, b_all.shape[2]))
    squares = total_over_all(squares, count, layers)
    entries = float(width * count * (width * count))
    rms_norm = jnp.sqrt(squares / entries + 1e-06)
    return (product, rms_norm)


def solution(mesh):
    placed = (P("row", "col"), P("row", "col"), P("row", "col"), P("row", "col"))
    return jax.shard_map(
        per_device,
        mesh=mesh,
        in_specs=placed,
        out_specs=(P("row", ("col", "depth")), P()),
        check_vma=False,
    )
```

```python
import functools

import jax
import jax.numpy as jnp
from jax import lax
from jax.experimental import pallas as pl
from jax.experimental.pallas import tpu as pltpu
from jax.sharding import PartitionSpec as P


def mask_kernel(layer_ref, mask_ref, matrix_ref, out_ref):
    blocks = mask_ref.shape[0]
    size = matrix_ref.shape[0] // blocks
    half = blocks // 2
    layer = layer_ref[0]
    for d in range(2):
        @pl.when(layer == d)
        def _(d=d):
            for i in range(blocks):
                for j in range(half):
                    k = d * half + j
                    tile = matrix_ref[i * size:(i + 1) * size, k * size:(k + 1) * size]
                    out_ref[i * size:(i + 1) * size, j * size:(j + 1) * size] = jnp.where(
                        mask_ref[i, k] != 0, tile, jnp.zeros_like(tile)
                    )


def masked_half(layer, mask, matrix):
    width = matrix.shape[0]
    smem = pl.BlockSpec(memory_space=pltpu.SMEM)
    vmem = pl.BlockSpec(memory_space=pltpu.VMEM)
    return pl.pallas_call(
        mask_kernel,
        in_specs=[smem, smem, vmem],
        out_specs=vmem,
        out_shape=jax.ShapeDtypeStruct((width, width // 2), matrix.dtype),
        compiler_params=pltpu.CompilerParams(vmem_limit_bytes=58 << 20),
        cost_estimate=pl.CostEstimate(
            flops=0, bytes_accessed=matrix.size * 3, transcendentals=0
        ),
    )(layer[None], mask, matrix)


def product_kernel(ahead, a_ref, b_ref, out_ref, squares_ref, a_held, b_held, a_came, b_came):
    count, rows = a_ref.shape[0], a_ref.shape[1] // 2

    def copies(n):
        return (
            pltpu.make_async_copy(b_ref.at[n], b_held.at[n], b_came.at[n]),
            pltpu.make_async_copy(a_ref.at[n], a_held.at[n], a_came.at[n]),
        )

    for n in range(min(ahead, count)):
        for copy in copies(n):
            copy.start()
    totals = [None, None]
    for n in range(count):
        for copy in copies(n):
            copy.wait()
        if n + ahead < count:
            for copy in copies(n + ahead):
                copy.start()
        for h in range(2):
            part = jnp.dot(
                a_held[n, h * rows:(h + 1) * rows], b_held[n],
                preferred_element_type=jnp.float32,
            )
            totals[h] = part if totals[h] is None else totals[h] + part
    squares = None
    for h, total in enumerate(totals):
        out_ref[h * rows:(h + 1) * rows] = total.astype(out_ref.dtype)
        more = jnp.sum(jnp.square(total).reshape(-1, 8, total.shape[1]), 0)
        squares = more if squares is None else squares + more
    squares = jnp.sum(squares[:, :128] + squares[:, 128:], 0, keepdims=True)
    squares_ref[...] = jnp.broadcast_to(squares[None], squares_ref.shape)


def multiply(a_all, b_all, copies):
    count, rows, depth = a_all.shape
    cols = b_all.shape[2]
    vmem = pl.BlockSpec(memory_space=pltpu.VMEM)
    return pl.pallas_call(
        functools.partial(product_kernel, 12),
        in_specs=[pl.BlockSpec(memory_space=pl.ANY)] * 2,
        out_specs=[vmem, vmem],
        out_shape=[
            jax.ShapeDtypeStruct((rows, cols), a_all.dtype),
            jax.ShapeDtypeStruct((copies, 1, 128), jnp.float32),
        ],
        scratch_shapes=[
            pltpu.VMEM(a_all.shape, a_all.dtype),
            pltpu.VMEM(b_all.shape, b_all.dtype),
            pltpu.SemaphoreType.DMA((count,)),
            pltpu.SemaphoreType.DMA((count,)),
        ],
        compiler_params=pltpu.CompilerParams(vmem_limit_bytes=57 << 20),
        cost_estimate=pl.CostEstimate(
            flops=2 * count * rows * depth * cols,
            bytes_accessed=2 * (a_all.size + b_all.size),
            transcendentals=0,
        ),
    )(a_all, b_all)


def near_runs(count, layers, near):
    return [
        [(r * count + run * near + c) * layers + d
         for r in range(count) for c in range(near) for d in range(layers)]
        for run in range(count // near)
    ]


def total_over_all(copies, count, runs, near):
    value = jnp.sum(
        lax.all_to_all(
            copies, ("row", "col", "depth"), 0, 0, tiled=True, axis_index_groups=runs
        ), 0
    )
    apart = [[run * near + c for run in range(len(runs))] for c in range(near)]
    return jnp.sum(lax.all_gather(value, "col", axis_index_groups=apart), (0, 1, 2))


def per_device(a_matrix, b_matrix, mask_a, mask_b):
    layer = lax.axis_index("depth")
    layers = lax.axis_size("depth")
    count = lax.axis_size("row")
    width = a_matrix.shape[0]
    a_part = masked_half(layer, mask_a, a_matrix)
    a_all = lax.all_gather(a_part, ("col", "depth"), axis=0)
    b_part = masked_half(layer, mask_b, b_matrix)
    copies = jnp.broadcast_to(b_part, (count,) + b_part.shape)
    b_all = lax.all_to_all(copies, "row", 0, 0, tiled=True)
    b_all = b_all.reshape(a_all.shape[0], -1, b_all.shape[2])
    near = 4
    runs = near_runs(count, layers, near)
    product, copies = multiply(a_all, b_all, len(runs[0]))
    squares = total_over_all(copies, count, runs, near)
    entries = float(width * count * (width * count))
    rms_norm = jnp.sqrt(squares / entries + 1e-06)
    return (product, rms_norm)


def solution(mesh):
    placed = (P("row", "col"), P("row", "col"), P("row", "col"), P("row", "col"))
    return jax.shard_map(
        per_device,
        mesh=mesh,
        in_specs=placed,
        out_specs=(P("row", ("col", "depth")), P()),
        check_vma=False,
    )
```

```python
import functools

import jax
import jax.numpy as jnp
from jax import lax
from jax.experimental import pallas as pl
from jax.experimental.pallas import tpu as pltpu
from jax.sharding import PartitionSpec as P


def mask_kernel(layer_ref, mask_ref, matrix_ref, out_ref):
    blocks = mask_ref.shape[0]
    size = matrix_ref.shape[0] // blocks
    half = blocks // 2
    layer = layer_ref[0]
    for d in range(2):
        @pl.when(layer == d)
        def _(d=d):
            for i in range(blocks):
                for j in range(half):
                    k = d * half + j
                    tile = matrix_ref[i * size:(i + 1) * size, k * size:(k + 1) * size]
                    out_ref[i * size:(i + 1) * size, j * size:(j + 1) * size] = jnp.where(
                        mask_ref[i, k] != 0, tile, jnp.zeros_like(tile)
                    )


def masked_half(layer, mask, matrix):
    width = matrix.shape[0]
    smem = pl.BlockSpec(memory_space=pltpu.SMEM)
    vmem = pl.BlockSpec(memory_space=pltpu.VMEM)
    return pl.pallas_call(
        mask_kernel,
        in_specs=[smem, smem, vmem],
        out_specs=vmem,
        out_shape=jax.ShapeDtypeStruct((width, width // 2), matrix.dtype),
        compiler_params=pltpu.CompilerParams(vmem_limit_bytes=58 << 20),
        cost_estimate=pl.CostEstimate(
            flops=0, bytes_accessed=matrix.size * 3, transcendentals=0
        ),
    )(layer[None], mask, matrix)


def product_kernel(group, a_ref, b_ref, out_ref, squares_ref, a_held, b_held, a_came, b_came):
    count, rows = a_ref.shape[0], a_ref.shape[1] // 2

    def copies(first):
        some = pl.ds(first, group)
        return (
            pltpu.make_async_copy(b_ref.at[some], b_held.at[some], b_came.at[first // group]),
            pltpu.make_async_copy(a_ref.at[some], a_held.at[some], a_came.at[first // group]),
        )

    for first in range(0, count, group):
        for copy in copies(first):
            copy.start()
    totals = [None, None]
    for n in range(count):
        if n % group == 0:
            for copy in copies(n):
                copy.wait()
        for h in range(2):
            part = jnp.dot(
                a_held[n, h * rows:(h + 1) * rows], b_held[n],
                preferred_element_type=jnp.float32,
            )
            totals[h] = part if totals[h] is None else totals[h] + part
    squares = None
    for h, total in enumerate(totals):
        out_ref[h * rows:(h + 1) * rows] = total.astype(out_ref.dtype)
        more = jnp.sum(jnp.square(total).reshape(-1, 8, total.shape[1]), 0)
        squares = more if squares is None else squares + more
    squares = jnp.sum(squares[:, :128] + squares[:, 128:], 0, keepdims=True)
    squares_ref[...] = jnp.broadcast_to(squares[None], squares_ref.shape)


def multiply(a_all, b_all, copies):
    count, rows, depth = a_all.shape
    cols = b_all.shape[2]
    vmem = pl.BlockSpec(memory_space=pltpu.VMEM)
    return pl.pallas_call(
        functools.partial(product_kernel, 2),
        in_specs=[pl.BlockSpec(memory_space=pl.ANY)] * 2,
        out_specs=[vmem, vmem],
        out_shape=[
            jax.ShapeDtypeStruct((rows, cols), a_all.dtype),
            jax.ShapeDtypeStruct((copies, 1, 128), jnp.float32),
        ],
        scratch_shapes=[
            pltpu.VMEM(a_all.shape, a_all.dtype),
            pltpu.VMEM(b_all.shape, b_all.dtype),
            pltpu.SemaphoreType.DMA((count,)),
            pltpu.SemaphoreType.DMA((count,)),
        ],
        compiler_params=pltpu.CompilerParams(vmem_limit_bytes=57 << 20),
        cost_estimate=pl.CostEstimate(
            flops=2 * count * rows * depth * cols,
            bytes_accessed=2 * (a_all.size + b_all.size),
            transcendentals=0,
        ),
    )(a_all, b_all)


def near_runs(count, layers, near):
    return [
        [(r * count + run * near + c) * layers + d
         for r in range(count) for c in range(near) for d in range(layers)]
        for run in range(count // near)
    ]


def total_over_all(copies, count, runs, near):
    value = jnp.sum(
        lax.all_to_all(
            copies, ("row", "col", "depth"), 0, 0, tiled=True, axis_index_groups=runs
        ), 0
    )
    apart = [[run * near + c for run in range(len(runs))] for c in range(near)]
    return jnp.sum(lax.all_gather(value, "col", axis_index_groups=apart), (0, 1, 2))


def per_device(a_matrix, b_matrix, mask_a, mask_b):
    layer = lax.axis_index("depth")
    layers = lax.axis_size("depth")
    count = lax.axis_size("row")
    width = a_matrix.shape[0]
    a_part = masked_half(layer, mask_a, a_matrix)
    a_all = lax.all_gather(a_part, ("col", "depth"), axis=0)
    b_part = masked_half(layer, mask_b, b_matrix)
    copies = jnp.broadcast_to(b_part, (count,) + b_part.shape)
    b_all = lax.all_to_all(copies, "row", 0, 0, tiled=True)
    b_all = b_all.reshape(a_all.shape[0], -1, b_all.shape[2])
    near = 4
    runs = near_runs(count, layers, near)
    product, copies = multiply(a_all, b_all, len(runs[0]))
    squares = total_over_all(copies, count, runs, near)
    entries = float(width * count * (width * count))
    rms_norm = jnp.sqrt(squares / entries + 1e-06)
    return (product, rms_norm)


def solution(mesh):
    placed = (P("row", "col"), P("row", "col"), P("row", "col"), P("row", "col"))
    return jax.shard_map(
        per_device,
        mesh=mesh,
        in_specs=placed,
        out_specs=(P("row", ("col", "depth")), P()),
        check_vma=False,
    )
```

```python
import functools

import jax
import jax.numpy as jnp
from jax import lax
from jax.experimental import pallas as pl
from jax.experimental.pallas import tpu as pltpu
from jax.sharding import PartitionSpec as P


def mask_kernel(layer_ref, mask_ref, matrix_ref, out_ref):
    blocks = mask_ref.shape[0]
    size = matrix_ref.shape[0] // blocks
    half = blocks // 2
    layer = layer_ref[0]
    for d in range(2):
        @pl.when(layer == d)
        def _(d=d):
            for i in range(blocks):
                for j in range(half):
                    k = d * half + j
                    tile = matrix_ref[i * size:(i + 1) * size, k * size:(k + 1) * size]
                    out_ref[i * size:(i + 1) * size, j * size:(j + 1) * size] = jnp.where(
                        mask_ref[i, k] != 0, tile, jnp.zeros_like(tile)
                    )


def masked_half(layer, mask, matrix):
    width = matrix.shape[0]
    smem = pl.BlockSpec(memory_space=pltpu.SMEM)
    vmem = pl.BlockSpec(memory_space=pltpu.VMEM)
    return pl.pallas_call(
        mask_kernel,
        in_specs=[smem, smem, vmem],
        out_specs=vmem,
        out_shape=jax.ShapeDtypeStruct((width, width // 2), matrix.dtype),
        compiler_params=pltpu.CompilerParams(vmem_limit_bytes=58 << 20),
        cost_estimate=pl.CostEstimate(
            flops=0, bytes_accessed=matrix.size * 3, transcendentals=0
        ),
    )(layer[None], mask, matrix)


def product_kernel(group, a_ref, b_ref, out_ref, squares_ref, a_held, b_held, a_came, b_came):
    count, rows = a_ref.shape[0], a_ref.shape[1] // 2

    sizes = [1, 1] + [group] * ((count - 2) // group)
    firsts = {sum(sizes[:m]): m for m in range(len(sizes))}

    def copies(first):
        m = firsts[first]
        some = pl.ds(first, sizes[m])
        return (
            pltpu.make_async_copy(b_ref.at[some], b_held.at[some], b_came.at[m]),
            pltpu.make_async_copy(a_ref.at[some], a_held.at[some], a_came.at[m]),
        )

    for first in firsts:
        for copy in copies(first):
            copy.start()
    totals = [None, None]
    for n in range(count):
        if n in firsts:
            for copy in copies(n):
                copy.wait()
        for h in range(2):
            part = jnp.dot(
                a_held[n, h * rows:(h + 1) * rows], b_held[n],
                preferred_element_type=jnp.float32,
            )
            totals[h] = part if totals[h] is None else totals[h] + part
    squares = None
    for h, total in enumerate(totals):
        out_ref[h * rows:(h + 1) * rows] = total.astype(out_ref.dtype)
        more = jnp.sum(jnp.square(total).reshape(-1, 8, total.shape[1]), 0)
        squares = more if squares is None else squares + more
    squares = jnp.sum(squares[:, :128] + squares[:, 128:], 0, keepdims=True)
    squares_ref[...] = jnp.broadcast_to(squares[None], squares_ref.shape)


def multiply(a_all, b_all, copies):
    count, rows, depth = a_all.shape
    cols = b_all.shape[2]
    vmem = pl.BlockSpec(memory_space=pltpu.VMEM)
    return pl.pallas_call(
        functools.partial(product_kernel, 2),
        in_specs=[pl.BlockSpec(memory_space=pl.ANY)] * 2,
        out_specs=[vmem, vmem],
        out_shape=[
            jax.ShapeDtypeStruct((rows, cols), a_all.dtype),
            jax.ShapeDtypeStruct((copies, 1, 128), jnp.float32),
        ],
        scratch_shapes=[
            pltpu.VMEM(a_all.shape, a_all.dtype),
            pltpu.VMEM(b_all.shape, b_all.dtype),
            pltpu.SemaphoreType.DMA((count,)),
            pltpu.SemaphoreType.DMA((count,)),
        ],
        compiler_params=pltpu.CompilerParams(vmem_limit_bytes=57 << 20),
        cost_estimate=pl.CostEstimate(
            flops=2 * count * rows * depth * cols,
            bytes_accessed=2 * (a_all.size + b_all.size),
            transcendentals=0,
        ),
    )(a_all, b_all)


def near_runs(count, layers, near):
    return [
        [(r * count + run * near + c) * layers + d
         for r in range(count) for c in range(near) for d in range(layers)]
        for run in range(count // near)
    ]


def total_over_all(copies, count, runs, near):
    value = jnp.sum(
        lax.all_to_all(
            copies, ("row", "col", "depth"), 0, 0, tiled=True, axis_index_groups=runs
        ), 0
    )
    apart = [[run * near + c for run in range(len(runs))] for c in range(near)]
    return jnp.sum(lax.all_gather(value, "col", axis_index_groups=apart), (0, 1, 2))


def per_device(a_matrix, b_matrix, mask_a, mask_b):
    layer = lax.axis_index("depth")
    layers = lax.axis_size("depth")
    count = lax.axis_size("row")
    width = a_matrix.shape[0]
    a_part = masked_half(layer, mask_a, a_matrix)
    a_all = lax.all_gather(a_part, ("col", "depth"), axis=0)
    b_part = masked_half(layer, mask_b, b_matrix)
    copies = jnp.broadcast_to(b_part, (count,) + b_part.shape)
    b_all = lax.all_to_all(copies, "row", 0, 0, tiled=True)
    b_all = b_all.reshape(a_all.shape[0], -1, b_all.shape[2])
    near = 4
    runs = near_runs(count, layers, near)
    product, copies = multiply(a_all, b_all, len(runs[0]))
    squares = total_over_all(copies, count, runs, near)
    entries = float(width * count * (width * count))
    rms_norm = jnp.sqrt(squares / entries + 1e-06)
    return (product, rms_norm)


def solution(mesh):
    placed = (P("row", "col"), P("row", "col"), P("row", "col"), P("row", "col"))
    return jax.shard_map(
        per_device,
        mesh=mesh,
        in_specs=placed,
        out_specs=(P("row", ("col", "depth")), P()),
        check_vma=False,
    )
```

```python
import functools

import jax
import jax.numpy as jnp
from jax import lax
from jax.experimental import pallas as pl
from jax.experimental.pallas import tpu as pltpu
from jax.sharding import PartitionSpec as P


def mask_kernel(layer_ref, mask_ref, matrix_ref, out_ref):
    blocks = mask_ref.shape[0]
    size = matrix_ref.shape[0] // blocks
    half = blocks // 2
    layer = layer_ref[0]
    for d in range(2):
        @pl.when(layer == d)
        def _(d=d):
            for i in range(blocks):
                for j in range(half):
                    k = d * half + j
                    tile = matrix_ref[i * size:(i + 1) * size, k * size:(k + 1) * size]
                    out_ref[i * size:(i + 1) * size, j * size:(j + 1) * size] = jnp.where(
                        mask_ref[i, k] != 0, tile, jnp.zeros_like(tile)
                    )


def masked_half(layer, mask, matrix):
    width = matrix.shape[0]
    smem = pl.BlockSpec(memory_space=pltpu.SMEM)
    vmem = pl.BlockSpec(memory_space=pltpu.VMEM)
    return pl.pallas_call(
        mask_kernel,
        in_specs=[smem, smem, vmem],
        out_specs=vmem,
        out_shape=jax.ShapeDtypeStruct((width, width // 2), matrix.dtype),
        compiler_params=pltpu.CompilerParams(vmem_limit_bytes=58 << 20),
        cost_estimate=pl.CostEstimate(
            flops=0, bytes_accessed=matrix.size * 3, transcendentals=0
        ),
    )(layer[None], mask, matrix)


def product_kernel(group, a_ref, b_ref, out_ref, squares_ref, a_held, b_held, a_came, b_came):
    count, rows = a_ref.shape[0], a_ref.shape[1] // 2

    def copies(first):
        some = pl.ds(first, group)
        return (
            pltpu.make_async_copy(b_ref.at[some], b_held.at[some], b_came.at[first // group]),
            pltpu.make_async_copy(a_ref.at[some], a_held.at[some], a_came.at[first // group]),
        )

    for first in range(0, count, group):
        for copy in copies(first):
            copy.start()
    totals = [None, None]
    for n in range(count):
        if n % group == 0:
            for copy in copies(n):
                copy.wait()
        for h in range(2):
            part = jnp.dot(
                a_held[n, h * rows:(h + 1) * rows], b_held[n],
                preferred_element_type=jnp.float32,
            )
            totals[h] = part if totals[h] is None else totals[h] + part
    squares = None
    for h, total in enumerate(totals):
        out_ref[h * rows:(h + 1) * rows] = total.astype(out_ref.dtype)
        more = jnp.sum(jnp.square(total).reshape(-1, 8, total.shape[1]), 0)
        squares = more if squares is None else squares + more
    squares = jnp.sum(squares[:, :128] + squares[:, 128:], 0, keepdims=True)
    squares_ref[...] = jnp.broadcast_to(squares[None], squares_ref.shape)


def multiply(a_all, b_all, copies):
    count, rows, depth = a_all.shape
    cols = b_all.shape[2]
    vmem = pl.BlockSpec(memory_space=pltpu.VMEM)
    return pl.pallas_call(
        functools.partial(product_kernel, 2),
        in_specs=[pl.BlockSpec(memory_space=pl.ANY)] * 2,
        out_specs=[vmem, vmem],
        out_shape=[
            jax.ShapeDtypeStruct((rows, cols), a_all.dtype),
            jax.ShapeDtypeStruct((copies, 1, 128), jnp.float32),
        ],
        scratch_shapes=[
            pltpu.VMEM(a_all.shape, a_all.dtype),
            pltpu.VMEM(b_all.shape, b_all.dtype),
            pltpu.SemaphoreType.DMA((count,)),
            pltpu.SemaphoreType.DMA((count,)),
        ],
        compiler_params=pltpu.CompilerParams(vmem_limit_bytes=57 << 20),
        cost_estimate=pl.CostEstimate(
            flops=2 * count * rows * depth * cols,
            bytes_accessed=2 * (a_all.size + b_all.size),
            transcendentals=0,
        ),
    )(a_all, b_all)


def near_runs(count, layers, near):
    return [
        [(r * count + run * near + c) * layers + d
         for r in range(count) for c in range(near) for d in range(layers)]
        for run in range(count // near)
    ]


def total_over_all(copies, count, runs, near):
    value = jnp.sum(
        lax.all_to_all(
            copies, ("row", "col", "depth"), 0, 0, tiled=True, axis_index_groups=runs
        ), 0
    )
    apart = [[run * near + c for run in range(len(runs))] for c in range(near)]
    return jnp.sum(lax.all_gather(value, "col", axis_index_groups=apart), (0, 1, 2))


def per_device(a_matrix, b_matrix, mask_a, mask_b):
    layer = lax.axis_index("depth")
    layers = lax.axis_size("depth")
    count = lax.axis_size("row")
    width = a_matrix.shape[0]
    a_part = masked_half(layer, mask_a, a_matrix)
    a_all = lax.all_gather(a_part, ("col", "depth"), axis=0)
    b_part = masked_half(layer, mask_b, b_matrix)
    copies = jnp.broadcast_to(b_part, (count,) + b_part.shape)
    b_all = lax.all_to_all(copies, "row", 0, 0, tiled=True)
    b_all = b_all.reshape(a_all.shape[0], -1, b_all.shape[2])
    near = 2
    runs = near_runs(count, layers, near)
    product, copies = multiply(a_all, b_all, len(runs[0]))
    squares = total_over_all(copies, count, runs, near)
    entries = float(width * count * (width * count))
    rms_norm = jnp.sqrt(squares / entries + 1e-06)
    return (product, rms_norm)


def solution(mesh):
    placed = (P("row", "col"), P("row", "col"), P("row", "col"), P("row", "col"))
    return jax.shard_map(
        per_device,
        mesh=mesh,
        in_specs=placed,
        out_specs=(P("row", ("col", "depth")), P()),
        check_vma=False,
    )
```
